32 devices in a mesh: space: 8 (over z, core), mode: 4 (over y, x).
Axes of the slice: x: 2, y: 2, z: 4, core: 2. Of those that a mesh axis runs over, the one named last changes fastest.
Arguments:
- guess: float32 [4096, 2048], P('space', 'mode'), may hold values from -6 to 6
- forcing: float32 [4096, 2048], P('space', 'mode'), may hold values from -6 to 6
- spatial_diag: bfloat16 [4096, 512], P('space'), may hold values from -0.25 to 0.25
- spatial_ghost: bfloat16 [4096, 256], P('space'), may hold values from -0.375 to 0.375
- ghost_rows: int32 [16, 128], P('space'), may hold values from 0 to 511, as said below
- chaos_vals: bfloat16 [128, 128, 128], P('mode'), may hold values from -0.25 to 0.25
- chaos_targets: int32 [16, 8], replicated, may hold values from 0 to 15, as said below
- chaos_count: int32 [16], replicated, may hold values from 1 to 8, as said below
- mean_inverse: bfloat16 [2048, 2048], replicated, may hold values from -0.125 to 0.125
Outputs:
- field: float32 [4096, 2048], P('space', 'mode')
The draws below stay inside these ranges and needn't reach their ends.
Inputs may be any that keep to these rules, and one draw needn't show every extreme that they name: `ghost_rows`: each row holds 128 distinct node numbers, 0 and 511 among them. `chaos_targets`: the targets in a row are distinct and the first is the row's own chaos block. Only the first chaos_count[j] slots of row j are used; some row uses all 8 slots and some row only one.
All inputs are finite; a program needn't handle non-finite values.
Results may differ from the reference program's by a relative error of at most 0.0021.
Values may be sent and summed in bfloat16 or wider, within the bound.
No kernel may reach another device: no remote copies, remote signals or barrier semaphores. Data moves between devices by JAX's collectives and lax.ppermute only.
A program may use at most 128 MiB of HBM per device.

```python
import jax
import jax.numpy as jnp
from jax import lax

NODE_DEV = 512
GHOST = 128
MODES = 2048
CB = 128
LIST = 8
ITERS = 3
NODES = 4096


def chaos_lists(key):
    mode_blocks = MODES // CB
    base = jax.random.fold_in(key, 71)
    keys = jax.random.split(base, mode_blocks + 3)

    def offsets_for(sub_key):
        return jax.random.permutation(sub_key, mode_blocks - 1)[:LIST - 1].astype(jnp.int32) + 1
    offsets = jax.vmap(offsets_for)(keys[:mode_blocks])
    own = jnp.arange(mode_blocks, dtype=jnp.int32)[:, None]
    steps_away = jnp.concatenate([jnp.zeros((mode_blocks, 1), jnp.int32), offsets], axis=1)
    targets = (own + steps_away) % mode_blocks
    first_draw = jax.random.randint(keys[mode_blocks], (mode_blocks,), 1, LIST + 1)
    second_draw = jax.random.randint(keys[mode_blocks + 1], (mode_blocks,), 1, LIST + 1)
    counts = jnp.minimum(first_draw, second_draw).astype(jnp.int32)
    fullest = jax.random.randint(keys[mode_blocks + 2], (), 0, mode_blocks)
    counts = counts.at[fullest].set(LIST)
    counts = counts.at[(fullest + 1) % mode_blocks].set(1)
    return (targets.astype(jnp.int32), counts.astype(jnp.int32))


def draw_chaos_targets(key, part):
    return chaos_lists(key)[0]


def draw_chaos_count(key, part):
    return chaos_lists(key)[1]


def draw_ghost_rows(key, part):
    list_count = 2 * (NODES // NODE_DEV)
    keys = jax.random.split(jax.random.fold_in(key, 13), list_count)

    def one_list(sub_key):
        first_key, second_key = jax.random.split(sub_key)
        inner = jax.random.permutation(first_key, NODE_DEV - 2)[:GHOST - 2].astype(jnp.int32) + 1
        chosen = jnp.concatenate([jnp.array([0, NODE_DEV - 1], jnp.int32), inner])
        return chosen[jax.random.permutation(second_key, GHOST)]
    return jax.vmap(one_list)(keys).astype(jnp.int32)


def shard_levels(stream_key, shape, pieces, least, largest):
    def one(axis_at, parts):
        heights = jax.random.uniform(jax.random.fold_in(jax.random.fold_in(stream_key, 6), axis_at), (parts,), jnp.float32, least / len(pieces), largest / len(pieces))
        return jnp.repeat(jnp.exp(heights), shape[axis_at] // parts).reshape((-1,) + (1,) * (len(shape) - axis_at - 1))

    level = one(*pieces[0])
    for cut in pieces[1:]:
        level = level * one(*cut)
    return level


def centred(key, shape, spread, limit, cuts=(), kind=jnp.bfloat16):
    entries = jax.random.normal(key, shape, jnp.float32) * spread
    if len(cuts) > 0:
        entries = shard_levels(key, shape, cuts, -0.22, 0.18) * entries
    return jnp.clip(entries, min=-limit, max=limit).astype(kind)


def setup_inputs(seed: int = 0) -> dict:
    key_of = jax.random.split(jax.random.key(seed), 10)
    return {
        "guess": centred(key_of[0], (NODES, MODES), 1.0, 6.0, ((0, 8), (1, 4)), jnp.float32),
        "forcing": centred(key_of[1], (NODES, MODES), 1.0, 6.0, ((0, 8), (1, 4)), jnp.float32),
        "spatial_diag": centred(key_of[2], (NODES, NODE_DEV), NODE_DEV ** -0.5, 0.25, ((0, 8),)),
        "spatial_ghost": centred(key_of[3], (NODES, 2 * GHOST), (2 * GHOST) ** -0.5, 0.375, ((0, 8),)),
        "ghost_rows": draw_ghost_rows(jax.random.fold_in(key_of[9], 71), 0),
        "chaos_vals": centred(key_of[5], (MODES // CB * LIST, CB, CB), (4 * CB) ** -0.5, 0.25, ((0, 4),)),
        "chaos_targets": draw_chaos_targets(jax.random.fold_in(key_of[9], 71), 0),
        "chaos_count": draw_chaos_count(jax.random.fold_in(key_of[9], 71), 0),
        "mean_inverse": centred(key_of[8], (MODES, MODES), MODES ** -0.5, 0.125),
    }


step_gain = 0.5

def reference(guess, forcing, spatial_diag, spatial_ghost, ghost_rows, chaos_vals, chaos_targets, chaos_count, mean_inverse):
    space_blocks = NODES // NODE_DEV
    mode_blocks = MODES // CB
    indices = ghost_rows.reshape(space_blocks, 2, GHOST).astype(jnp.int32)
    diag_full = spatial_diag.astype(jnp.float32).reshape(space_blocks, NODE_DEV, NODE_DEV)
    ghost_full = spatial_ghost.astype(jnp.float32).reshape(space_blocks, NODE_DEV, 2 * GHOST)
    inverse_full = mean_inverse.astype(jnp.float32)
    values_full = chaos_vals.astype(jnp.float32).reshape(mode_blocks, LIST, CB, CB)
    field = guess
    for iteration in range(ITERS):
        field_low = lax.optimization_barrier(field.astype(jnp.bfloat16)).astype(jnp.float32)
        blocks = field_low.reshape(space_blocks, NODE_DEV, MODES)
        lower_sent = jnp.take_along_axis(blocks, indices[:, 0, :, None], axis=1)
        upper_sent = jnp.take_along_axis(blocks, indices[:, 1, :, None], axis=1)
        empty = jnp.zeros((1, GHOST, MODES), jnp.float32)
        from_below = jnp.concatenate([empty, upper_sent[:-1]], axis=0)
        from_above = jnp.concatenate([lower_sent[1:], empty], axis=0)
        ghosts = jnp.concatenate([from_below, from_above], axis=1)
        spatial = jnp.einsum('bij,bjm->bim', diag_full, blocks, precision=lax.Precision.HIGHEST)
        spatial = spatial + jnp.einsum('bij,bjm->bim', ghost_full, ghosts, precision=lax.Precision.HIGHEST)
        spatial = spatial.reshape(NODES, MODES)
        columns = field_low.reshape(NODES, mode_blocks, CB)

        def add_pair(pair, coupled):
            pair = jnp.asarray(pair).astype(jnp.int32)
            source_block = pair // LIST
            slot = pair % LIST
            target = chaos_targets[source_block, slot].astype(jnp.int32)
            active = (slot < chaos_count[source_block]).astype(jnp.float32)
            source = lax.dynamic_index_in_dim(columns, source_block, 1, keepdims=False)
            product = jnp.dot(source, values_full[source_block, slot].T, precision=lax.Precision.HIGHEST) * active
            current = lax.dynamic_index_in_dim(coupled, target, 1, keepdims=False)
            return lax.dynamic_update_index_in_dim(coupled, current + product, target, 1)
        coupled = lax.fori_loop(0, mode_blocks * LIST, add_pair, jnp.zeros((NODES, mode_blocks, CB), jnp.float32))
        residual = forcing - spatial - coupled.reshape(NODES, MODES)
        residual_low = lax.optimization_barrier(residual.astype(jnp.bfloat16)).astype(jnp.float32)
        update = jnp.dot(residual_low, inverse_full.T, precision=lax.Precision.HIGHEST)
        damping = step_gain / jnp.sqrt(jnp.mean(update * update) + 1e-06)
        field = field + damping * update
    return field
```

```python
import functools

import jax
import jax.numpy as jnp
from jax import lax
from jax.experimental import pallas as pl
from jax.experimental.pallas import tpu as pltpu
from jax.sharding import PartitionSpec as P


step_gain = 0.5
F32 = jnp.float32
BF16 = jnp.bfloat16
VMEM = pl.BlockSpec(memory_space=pltpu.VMEM)
SMEM = pl.BlockSpec(memory_space=pltpu.SMEM)


def call(body, outs, args, scalars=0, limit=40):
    return pl.pallas_call(
        body,
        out_shape=outs,
        in_specs=[SMEM] * scalars + [VMEM] * (len(args) - scalars),
        out_specs=[VMEM] * len(outs),
        compiler_params=pltpu.CompilerParams(vmem_limit_bytes=limit << 20),
    )(*args)


def shaped(shape, dtype=BF16):
    return jax.ShapeDtypeStruct(shape, dtype)


def rows_of(owner, rows):
    return pl.ds(pl.multiple_of(owner * rows, rows), rows)


def mm(a, b):
    return jnp.dot(a, b, preferred_element_type=F32)


def mmt(a, b):
    return lax.dot_general(a, b, (((1,), (1,)), ((), ())), preferred_element_type=F32)


def flip_permute(x, axis, bit):
    return lax.ppermute(x, axis, [(i, i ^ bit) for i in range(lax.axis_size(axis))])


def trade(pieces):
    return [pieces[0]] + [flip_permute(p, "mode", k) for k, p in enumerate(pieces) if k > 0]


def halo(lower, upper):
    count = lax.axis_size("space")
    below = lax.ppermute(upper, "space", [(i, i + 1) for i in range(count - 1)])
    above = lax.ppermute(lower, "space", [(i + 1, i) for i in range(count - 1)])
    return below, above


def start_body(n, where, u_ref, pick_ref, *outs):
    whole, lower, upper = outs[:3]
    rows = u_ref.shape[0] // n
    ghost = lower.shape[0]
    whole[...] = u_ref[...].astype(BF16)
    picked = mm(pick_ref[...], whole[...]).astype(BF16)
    lower[...] = picked[:ghost]
    upper[...] = picked[ghost:]
    for k in range(n):
        outs[3 + k][0] = whole[rows_of(where[0] ^ k, rows), :]


def spatial_of(diag, ghostly, x, below, above):
    ghost = below.shape[0]
    y = mm(diag[...], x[...])
    y = y + mm(ghostly[:, :ghost], below[...])
    return y + mm(ghostly[:, ghost:], above[...])


def first_body(n, where, diag, ghostly, x, below, above, f_ref, pick_ref, *outs):
    both, lower, upper = outs[:3]
    nodes, width = x.shape
    rows = nodes // n
    ghost = lower.shape[0]
    s = spatial_of(diag, ghostly, x, below, above)
    p = f_ref[...] - s
    high = p.astype(BF16)
    both[:, :width] = s.astype(BF16)
    both[:, width:] = high
    low = outs[-1]
    low[...] = (p - high.astype(F32)).astype(BF16)
    picked = mm(pick_ref[...], both[...]).astype(BF16)
    lower[...] = picked[:ghost]
    upper[...] = picked[ghost:]
    for k in range(n):
        at = rows_of(where[0] ^ k, rows)
        outs[3 + k][0] = both[at, width:]
        outs[3 + k][1] = low[at, :]
        outs[3 + k][2] = both[at, :width]


def second_body(n, where, diag, ghostly, x, below, above, pick_ref, *outs):
    p1, lower, upper = outs[:3]
    nodes, width = p1.shape
    rows = nodes // n
    ghost = lower.shape[0]
    y = spatial_of(diag, ghostly, x, below, above).astype(BF16)
    p1[...] = y[:, width:]
    picked = mm(pick_ref[...], p1[...]).astype(BF16)
    lower[...] = picked[:ghost]
    upper[...] = picked[ghost:]
    s2 = outs[-1]
    s2[...] = y[:, :width]
    for k in range(n):
        at = rows_of(where[0] ^ k, rows)
        outs[3 + k][0] = s2[at, :]
        outs[3 + k][1] = p1[at, :]


def third_body(n, where, diag, ghostly, x, below, above, *outs):
    rows = x.shape[0] // n
    whole = outs[-1]
    whole[...] = spatial_of(diag, ghostly, x, below, above).astype(BF16)
    for k in range(n):
        outs[k][0] = whole[rows_of(where[0] ^ k, rows), :]


def table_body(n, slots, per, where, targets, counts, *refs):
    out = refs[-1]
    step = 256
    width = refs[0].shape[-1]

    def clear(i, carry):
        out[pl.ds(pl.multiple_of(i * step, step), step), :] = jnp.zeros(
            (step, out.shape[1]), out.dtype
        )
        return carry

    lax.fori_loop(0, out.shape[0] // step, clear, 0)
    quarter = refs[0].shape[1]
    bits = n.bit_length() - 1
    for which in range(4):
        core = where[1] if which < 2 else 1 - where[1]
        base = core * (2 * quarter) + (which % 2) * quarter
        for k in range(n):
            at = k if which % 2 == 0 else int(format(k, "b").zfill(bits)[::-1], 2) if bits else 0
            owner = where[0] ^ k

            def place(i, carry, which=which, at=at, owner=owner, base=base):
                entry = base + i
                source = owner * per + entry // slots
                slot = entry % slots

                @pl.when(slot < counts[source])
                def _():
                    target = targets[source, slot]
                    out[
                        pl.ds(pl.multiple_of(target * width, width), width),
                        pl.ds(pl.multiple_of(source * width, width), width),
                    ] = refs[which][at, i]

                return carry

            lax.fori_loop(0, quarter, place, 0)


def apply(n, me, get, table, emit):
    width = table.shape[0] // n
    for g in range(n):
        out_rows = rows_of(me ^ g, width)
        total = None
        for k in range(n):
            part = mmt(get(k), table[out_rows, rows_of(me ^ k, width)])
            total = part if total is None else total + part
        emit(g, total)


def damping_of(squares, cells):
    total = jnp.sum(squares[...], axis=0, keepdims=True)[:, :1]
    return step_gain / jnp.sqrt(total / cells + 1e-06)


def stage_a(n, where, *refs):
    us, ps = refs[:n], refs[n : 2 * n]
    chaos, inverse, w0, c1, ca0, squares, pair, quick = refs[2 * n :]
    me = where[0]
    rows = us[0].shape[1]

    def residual(g, value):
        r = ps[g][0].astype(F32) + ps[g][1].astype(F32) - value[:rows]
        high = r.astype(BF16)
        pair[g, :rows] = high
        pair[g, rows:] = (r - high.astype(F32)).astype(BF16)
        c1[g] = value[rows:]

    apply(n, me, lambda k: jnp.concatenate([us[k][0], ps[k][2]], axis=0), chaos, residual)
    sums = []

    def updated(g, value):
        w = value[:rows] + value[rows:]
        w0[g] = w
        quick[g] = w.astype(BF16)
        sums.append(jnp.sum(w * w))

    apply(n, me, lambda k: pair[k], inverse, updated)
    squares[...] = jnp.full(squares.shape, sum(sums), F32)

    def coupled(g, value):
        ca0[g] = value

    apply(n, me, lambda k: quick[k], chaos, coupled)


def stage_b(n, cells, where, *refs):
    ps = refs[:n]
    chaos, inverse, w0, c1, ca0, sq0, v1, w1, c2, ca1, cv1, squares, one, three = refs[n:]
    me = where[0]
    rows = w0.shape[1]
    d0 = damping_of(sq0, cells)

    for g in range(n):
        one[g] = (ps[g][1].astype(F32) - c1[g]).astype(BF16)
        three[g, :rows] = ps[g][0]

    def moved(g, value):
        three[g, rows : 2 * rows] = value.astype(BF16)
        v1[g] = value + ca0[g]

    apply(n, me, lambda k: one[k], inverse, moved)
    for g in range(n):
        one[g] = v1[g].astype(BF16)
    sums = []

    def updated(g, value):
        v1[g] = value
        three[g, 2 * rows :] = value.astype(BF16)
        w = w0[g] - d0 * value
        w1[g] = w
        sums.append(jnp.sum(w * w))

    apply(n, me, lambda k: one[k], inverse, updated)
    squares[...] = jnp.full(squares.shape, sum(sums), F32)

    def coupled(g, value):
        c2[g] = value[:rows]
        ca1[g] = value[rows : 2 * rows]
        cv1[g] = value[2 * rows :]

    apply(n, me, lambda k: three[k], chaos, coupled)


def mix_body(n, cells, w0, w1, sq0, sq1, *outs):
    d0 = damping_of(sq0, cells)
    d1 = damping_of(sq1, cells)
    for g in range(n):
        e = d0 * w0[g] + d1 * w1[g]
        high = e.astype(BF16)
        outs[g][0] = high
        outs[g][1] = (e - high.astype(F32)).astype(BF16)


def stage_c(n, cells, where, *refs):
    ps = refs[:n]
    inverse, v1, w1, c2, ca1, cv1, sq0, sq1 = refs[n : n + 8]
    outs = refs[n + 8 : 2 * n + 8]
    squares, one, two = refs[2 * n + 8 :]
    me = where[0]
    d0 = damping_of(sq0, cells)
    d1 = damping_of(sq1, cells)
    for g in range(n):
        one[g] = (ps[g][0].astype(F32) - c2[g]).astype(BF16)

    def second(g, value):
        two[g] = (value + ca1[g]).astype(BF16)

    apply(n, me, lambda k: one[k], inverse, second)

    def third(g, value):
        one[g] = (value + cv1[g]).astype(BF16)

    apply(n, me, lambda k: two[k], inverse, third)
    sums = []

    def last(g, value):
        w = w1[g] - d1 * (v1[g] - d0 * value)
        outs[g][...] = w.astype(BF16)
        sums.append(jnp.sum(w * w))

    apply(n, me, lambda k: one[k], inverse, last)
    squares[...] = jnp.full(squares.shape, sum(sums), F32)


def end_body(n, cells, where, u_ref, sq2, *refs):
    es, ws, out = refs[:n], refs[n : 2 * n], refs[2 * n]
    rows = u_ref.shape[0] // n
    d2 = damping_of(sq2, cells)
    for k in range(n):
        at = rows_of(where[0] ^ k, rows)
        e = es[k][0].astype(F32) + es[k][1].astype(F32)
        out[at, :] = u_ref[at, :] + (e + d2 * ws[k][...].astype(F32))


def summed(squares):
    return lax.all_to_all(squares, ("space", "mode"), split_axis=0, concat_axis=0, tiled=True)


def gathered(vals, core, n):
    entries = vals.shape[0]
    half = lax.dynamic_slice_in_dim(vals, core * (entries // 2), entries // 2, 0)
    bits = [1 << b for b in range(n.bit_length() - 1)]
    found = []
    for part, order in ((half[: entries // 4], bits), (half[entries // 4 :], bits[::-1])):
        held = part[None]
        for bit in order:
            held = jnp.concatenate([held, flip_permute(held, "mode", bit)], axis=0)
        found.append(held)
    return found + [flip_permute(held, "space", 1) for held in found]


def shards(
    guess,
    forcing,
    spatial_diag,
    spatial_ghost,
    ghost_rows,
    chaos_vals,
    chaos_targets,
    chaos_count,
    mean_inverse,
):
    n = lax.axis_size("mode")
    devices = n * lax.axis_size("space")
    nodes, width = guess.shape
    rows = nodes // n
    ghost = ghost_rows.shape[1]
    modes = mean_inverse.shape[0]
    slots = chaos_targets.shape[1]
    per = chaos_targets.shape[0] // n
    cells = float(nodes * width * devices)
    me = lax.axis_index("mode").astype(jnp.int32)
    core = (lax.axis_index("space") % 2).astype(jnp.int32)
    where = jnp.stack([me, core])
    pick = (ghost_rows.reshape(-1)[:, None] == jnp.arange(nodes, dtype=jnp.int32)[None, :]).astype(
        BF16
    )

    def sent(count):
        return [shaped((count, rows, width))] * n

    def edges(times):
        return [shaped((ghost, times * width))] * 2

    tables = gathered(chaos_vals, core, n)
    whole, lower, upper, *us = call(
        functools.partial(start_body, n),
        [shaped((nodes, width))] + edges(1) + sent(1),
        [where, guess, pick],
        1,
    )
    below, above = halo(lower, upper)
    us = trade(us)
    both, lower, upper, *ps = call(
        functools.partial(first_body, n),
        [shaped((nodes, 2 * width))] + edges(2) + sent(3) + [shaped((nodes, width))],
        [where, spatial_diag, spatial_ghost, whole, below, above, forcing, pick],
        1,
    )[:-1]
    below, above = halo(lower, upper)
    ps = trade(ps)
    p1, lower, upper, *qs = call(
        functools.partial(second_body, n),
        [shaped((nodes, width))] + edges(1) + sent(2) + [shaped((nodes, width))],
        [where, spatial_diag, spatial_ghost, both, below, above, pick],
        1,
    )[:-1]
    below, above = halo(lower, upper)
    qs = trade(qs)
    last = call(
        functools.partial(third_body, n),
        sent(1) + [shaped((nodes, width))],
        [where, spatial_diag, spatial_ghost, p1, below, above],
        1,
    )[:-1]
    last = trade(last)

    (chaos,) = call(
        functools.partial(table_body, n, slots, per),
        [shaped((modes, modes))],
        [where, chaos_targets, chaos_count] + tables,
        3,
    )
    slab = shaped((n, rows, width), F32)
    tile = shaped((devices, 128), F32)
    low_slab = shaped((n, rows, width))
    w0, c1, ca0, sq0 = call(
        functools.partial(stage_a, n),
        [slab, slab, slab, tile, shaped((n, 2 * rows, width)), low_slab],
        [where] + us + ps + [chaos, mean_inverse],
        1,
    )[:4]
    sq0 = summed(sq0)
    v1, w1, c2, ca1, cv1, sq1 = call(
        functools.partial(stage_b, n, cells),
        [slab, slab, slab, slab, slab, tile, low_slab, shaped((n, 3 * rows, width))],
        [where] + qs + [chaos, mean_inverse, w0, c1, ca0, sq0],
        1,
    )[:6]
    sq1 = summed(sq1)
    es = trade(call(functools.partial(mix_body, n, cells), sent(2), [w0, w1, sq0, sq1]))
    *ws, sq2 = call(
        functools.partial(stage_c, n, cells),
        [shaped((rows, width))] * n + [tile, low_slab, low_slab],
        [where] + last + [mean_inverse, v1, w1, c2, ca1, cv1, sq0, sq1],
        1,
    )[: n + 1]
    ws = trade(ws)
    sq2 = summed(sq2)
    (field,) = call(
        functools.partial(end_body, n, cells),
        [shaped((nodes, width), F32)],
        [where, guess, sq2] + es + ws,
        1,
    )
    return field


def solution(mesh):
    placed = (
        P("space", "mode"),
        P("space", "mode"),
        P("space", None),
        P("space", None),
        P("space", None),
        P("mode", None, None),
        P(),
        P(),
        P(),
    )
    return jax.shard_map(
        shards, mesh=mesh, in_specs=placed, out_specs=P("space", "mode"), check_vma=False
    )
```

```python
import functools

import jax
import jax.numpy as jnp
from jax import lax
from jax.experimental import pallas as pl
from jax.experimental.pallas import tpu as pltpu
from jax.sharding import PartitionSpec as P


step_gain = 0.5
F32 = jnp.float32
BF16 = jnp.bfloat16
VMEM = pl.BlockSpec(memory_space=pltpu.VMEM)
SMEM = pl.BlockSpec(memory_space=pltpu.SMEM)
HBM = pl.BlockSpec(memory_space=pltpu.HBM)


def call(body, outs, args, scalars=0, scratch=(), far=0, limit=16):
    far_at = slice(scalars, scalars + far)

    def whole(*refs):
        refs = list(refs)
        if far:
            sems = refs.pop()
            near = refs[len(refs) - far :]
            del refs[len(refs) - far :]
            copies = [
                pltpu.make_async_copy(a, b, sems.at[i])
                for i, (a, b) in enumerate(zip(refs[far_at], near))
            ]
            for copy in copies:
                copy.start()
            for copy in copies:
                copy.wait()
            refs[far_at] = near
        body(*refs)

    brought = [pltpu.VMEM(leaf.shape, leaf.dtype) for leaf in args[far_at]]
    return pl.pallas_call(
        whole,
        out_shape=outs,
        in_specs=[SMEM] * scalars
        + [HBM] * far
        + [VMEM] * (len(args) - scalars - far),
        out_specs=[VMEM] * len(outs),
        scratch_shapes=[pltpu.VMEM(leaf.shape, leaf.dtype) for leaf in scratch]
        + brought
        + ([pltpu.SemaphoreType.DMA((far,))] if far else []),
        compiler_params=pltpu.CompilerParams(vmem_limit_bytes=limit << 20),
        cost_estimate=pl.CostEstimate(flops=1, bytes_accessed=1, transcendentals=0),
    )(*args)


def shaped(shape, dtype=BF16):
    return jax.ShapeDtypeStruct(shape, dtype)


def rows_of(owner, rows):
    return pl.ds(pl.multiple_of(owner * rows, rows), rows)


def mm(a, b):
    return jnp.dot(a, b, preferred_element_type=F32)


def mmt(a, b):
    return lax.dot_general(a, b, (((1,), (1,)), ((), ())), preferred_element_type=F32)


def flip_permute(x, axis, bit):
    return lax.ppermute(x, axis, [(i, i ^ bit) for i in range(lax.axis_size(axis))])


def trade(pieces):
    return [pieces[0]] + [flip_permute(p, "mode", k) for k, p in enumerate(pieces) if k > 0]


def halo(lower, upper):
    count = lax.axis_size("space")
    below = lax.ppermute(upper, "space", [(i, i + 1) for i in range(count - 1)])
    above = lax.ppermute(lower, "space", [(i + 1, i) for i in range(count - 1)])
    return below, above


def picked_rows(pick, x, lower, upper):
    ghost = lower.shape[0]
    rows = mm(pick[...], x).astype(BF16)
    lower[...] = rows[:ghost]
    upper[...] = rows[ghost:]


def start_body(u_ref, pick, whole, lower, upper):
    whole[...] = u_ref[...].astype(BF16)
    picked_rows(pick, whole[...], lower, upper)


def spatial_of(diag, ghostly, x, below, above):
    ghost = below.shape[0]
    y = mm(diag[...], x[...])
    y = y + mm(ghostly[:, :ghost], below[...])
    return y + mm(ghostly[:, ghost:], above[...])


def first_body(n, where, diag, ghostly, f_ref, x, below, above, pick, *outs):
    both, lower, upper = outs[:3]
    low = outs[-1]
    nodes, width = x.shape
    s = spatial_of(diag, ghostly, x, below, above)
    p = f_ref[...] - s
    high = p.astype(BF16)
    both[:, :width] = s.astype(BF16)
    both[:, width:] = high
    low[...] = (p - high.astype(F32)).astype(BF16)
    picked_rows(pick, both[...], lower, upper)
    for k in range(n):
        at = rows_of(where[0] ^ k, nodes // n)
        outs[3 + k][0] = x[at, :]
        outs[3 + k][1] = both[at, width:]
        outs[3 + k][2] = low[at, :]
        outs[3 + k][3] = both[at, :width]


def second_body(diag, ghostly, x, below, above, pick, both, p1, lower, upper):
    both[...] = spatial_of(diag, ghostly, x, below, above).astype(BF16)
    p1[...] = both[:, both.shape[1] // 2 :]
    picked_rows(pick, p1[...], lower, upper)


def third_body(n, where, diag, ghostly, both, x, below, above, *outs):
    rows = x.shape[0] // n
    width = x.shape[1]
    whole = outs[-1]
    whole[...] = spatial_of(diag, ghostly, x, below, above).astype(BF16)
    for k in range(n):
        at = rows_of(where[0] ^ k, rows)
        outs[k][0] = both[at, :width]
        outs[k][1] = x[at, :]
        outs[k][2] = whole[at, :]


def table_body(n, slots, where, targets, counts, own, *refs):
    *refs, out = refs
    width = own.shape[-1]
    entries = own.shape[0]
    per = entries // slots
    quarter = entries // 4
    step = 256

    def clear(i, carry):
        out[rows_of(i, step), :] = jnp.zeros((step, out.shape[1]), out.dtype)
        return carry

    lax.fori_loop(0, out.shape[0] // step, clear, 0)

    def fill(owner, base, count, get):
        def place(i, carry):
            entry = base + i
            source = owner * per + entry // slots
            slot = entry % slots

            @pl.when(slot < counts[source])
            def _():
                out[rows_of(source, width), rows_of(targets[source, slot], width)] = get(i)

            return carry

        lax.fori_loop(0, count, place, 0)

    fill(where[0], 0, entries, lambda i: own[i])
    for which in range(4):
        for k in range(1, n):
            fill(
                where[0] ^ k,
                (where[1] ^ which) * quarter,
                quarter,
                lambda i, which=which, k=k: refs[which][k - 1, i],
            )


def by_table(n, me, get, table, emit):
    width = table.shape[0] // n
    for g in range(n):
        total = None
        for k in range(n):
            part = mm(get(k), table[rows_of(me ^ k, width), rows_of(me ^ g, width)])
            total = part if total is None else total + part
        emit(g, total)


def by_inverse(n, me, get, inverse, emit):
    width = inverse.shape[0] // n
    for g in range(n):
        total = None
        for k in range(n):
            part = mmt(get(k), inverse[rows_of(me ^ g, width), rows_of(me ^ k, width)])
            total = part if total is None else total + part
        emit(g, total)


def stage_a(n, where, *refs):
    ps = refs[:n]
    chaos, inverse, w0, c1, ca0 = refs[n : n + 5]
    outs = refs[n + 5 : 2 * n + 5]
    pair, quick = refs[2 * n + 5 :]
    me = where[0]
    rows = w0.shape[1]

    def residual(g, value):
        r = ps[g][1].astype(F32) + ps[g][2].astype(F32) - value[:rows]
        high = r.astype(BF16)
        pair[g, :rows] = high
        pair[g, rows:] = (r - high.astype(F32)).astype(BF16)
        c1[g] = value[rows:]

    by_table(n, me, lambda k: jnp.concatenate([ps[k][0], ps[k][3]], axis=0), chaos, residual)

    def updated(g, value):
        w = value[:rows] + value[rows:]
        w0[g] = w
        high = w.astype(BF16)
        quick[g] = high
        outs[g][0] = high
        outs[g][1] = (w - high.astype(F32)).astype(BF16)

    by_inverse(n, me, lambda k: pair[k], inverse, updated)

    def coupled(g, value):
        ca0[g] = value

    by_table(n, me, lambda k: quick[k], chaos, coupled)


def stage_b(n, where, *refs):
    qs = refs[:n]
    chaos, inverse, w0, c1, ca0 = refs[n : n + 5]
    outs = refs[n + 5 : 2 * n + 5]
    v1, held, sums_out, pair, more = refs[2 * n + 5 :]
    me = where[0]
    rows = w0.shape[1]
    for g in range(n):
        pair[g, :rows] = (qs[g][1].astype(F32) - c1[g]).astype(BF16)

    def residual(g, value):
        pair[g, rows:] = (qs[g][2].astype(F32) - value).astype(BF16)

    by_table(n, me, lambda k: qs[k][0], chaos, residual)

    def moved(g, value):
        more[g, :rows] = value[:rows].astype(BF16)
        held[g] = value[rows:]
        more[g, rows:] = (value[:rows] + ca0[g]).astype(BF16)

    by_inverse(n, me, lambda k: pair[k], inverse, moved)

    def coupled(g, value):
        pair[g, :rows] = more[g, rows:]
        pair[g, rows:] = (held[g] + value).astype(BF16)

    by_table(n, me, lambda k: more[k, :rows], chaos, coupled)
    sums = [0.0] * 3

    def first(g, value):
        v = value[:rows]
        v1[g] = v
        outs[g][0] = v.astype(BF16)
        held[g] = value[rows:]
        sums[0] += jnp.sum(w0[g] * w0[g])
        sums[1] += jnp.sum(w0[g] * v)
        sums[2] += jnp.sum(v * v)

    by_inverse(n, me, lambda k: pair[k], inverse, first)
    lanes_of(sums_out, sums, 0)


def lanes_of(out, sums, base):
    lane = lax.broadcasted_iota(jnp.int32, out.shape, 1)
    row = jnp.zeros(out.shape, F32)
    for at, value in enumerate(sums):
        row = jnp.where(lane == base + at, value, row)
    out[...] = row


def stage_c(n, where, chaos, inverse, w0, v1, held, sums_in, *refs):
    outs = refs[:n]
    dots, one, two = refs[n:]
    me = where[0]
    for g in range(n):
        one[g] = v1[g].astype(BF16)

    def last_in(g, value):
        two[g] = (held[g] + value).astype(BF16)

    by_table(n, me, lambda k: one[k], chaos, last_in)
    sums = [0.0] * 3

    def second(g, value):
        outs[g][0] = value.astype(BF16)
        sums[0] += jnp.sum(w0[g] * value)
        sums[1] += jnp.sum(v1[g] * value)
        sums[2] += jnp.sum(value * value)

    by_inverse(n, me, lambda k: two[k], inverse, second)
    lanes_of(dots, sums, 3)
    dots[...] = dots[...] + sums_in[...]


def end_body(n, cells, where, u_ref, dots, *refs):
    ws, vs, xs, out = refs[:n], refs[n : 2 * n], refs[2 * n : 3 * n], refs[3 * n]
    rows = u_ref.shape[0] // n
    means = jnp.sum(dots[...], axis=0, keepdims=True) / cells
    lane = lax.broadcasted_iota(jnp.int32, means.shape, 1)
    g00, g01, g11, g02, g12, g22 = [
        jnp.sum(jnp.where(lane == at, means, 0.0), axis=1, keepdims=True) for at in range(6)
    ]

    def damping(mean):
        return step_gain / jnp.sqrt(jnp.maximum(mean, 0.0) + 1e-06)

    d0 = damping(g00)
    d1 = damping(g00 - 2.0 * d0 * g01 + d0 * d0 * g11)
    a, b = d0 + d1, d0 * d1
    d2 = damping(
        g00 + a * a * g11 + b * b * g22 - 2.0 * a * g01 + 2.0 * b * g02 - 2.0 * a * b * g12
    )
    x0 = d0 + d1 + d2
    x1 = -(d1 * d0 + d2 * a)
    x2 = d2 * b
    for k in range(n):
        at = rows_of(where[0] ^ k, rows)
        w = ws[k][0].astype(F32) + ws[k][1].astype(F32)
        moved = x0 * w + x1 * vs[k][0].astype(F32) + x2 * xs[k][0].astype(F32)
        out[at, :] = u_ref[at, :] + moved


def gather_start(own, quarter, n):
    size = own.shape[0] // 4
    mine = lax.dynamic_slice_in_dim(own, quarter * size, size, 0)
    return [flip_permute(mine, "mode", k) for k in range(1, n)]


def gather_end(here, there):
    return [here, flip_permute(here, "space", 1), there, flip_permute(there, "space", 1)]


def shards(
    guess,
    forcing,
    spatial_diag,
    spatial_ghost,
    ghost_rows,
    chaos_vals,
    chaos_targets,
    chaos_count,
    mean_inverse,
):
    n = lax.axis_size("mode")
    devices = n * lax.axis_size("space")
    nodes, width = guess.shape
    rows = nodes // n
    ghost = ghost_rows.shape[1]
    modes = mean_inverse.shape[0]
    slots = chaos_targets.shape[1]
    cells = float(nodes * width * devices)
    me = lax.axis_index("mode").astype(jnp.int32)
    quarter = (lax.axis_index("space") % 4).astype(jnp.int32)
    where = jnp.stack([me, quarter])
    pick = (ghost_rows.reshape(-1)[:, None] == jnp.arange(nodes, dtype=jnp.int32)[None, :]).astype(
        BF16
    )

    def sent(count):
        return [shaped((count, rows, width))] * n

    def edges(times):
        return [shaped((ghost, times * width))] * 2

    one, two = shaped((nodes, width)), shaped((nodes, 2 * width))
    own = jnp.swapaxes(chaos_vals, 1, 2)
    pieces = gather_start(own, quarter, n)
    whole, lower, upper = call(start_body, [one] + edges(1), [guess, pick], far=1, limit=56)
    below, above = halo(lower, upper)
    both, lower, upper, *ps = call(
        functools.partial(first_body, n),
        [two] + edges(2) + sent(4),
        [where, spatial_diag, spatial_ghost, forcing, whole, below, above, pick],
        1,
        [one],
        3,
        56,
    )
    below, above = halo(lower, upper)
    ps = trade(ps)
    pieces, below, above = lax.optimization_barrier((pieces, below, above))
    here = jnp.stack(pieces)
    there = flip_permute(here, "space", 2)
    both, p1, lower, upper = call(
        second_body,
        [two, one] + edges(1),
        [spatial_diag, spatial_ghost, both, below, above, pick],
        far=2,
        limit=56,
    )
    below, above = halo(lower, upper)
    ps, below, above = lax.optimization_barrier((ps, below, above))
    qs = call(
        functools.partial(third_body, n),
        sent(3),
        [where, spatial_diag, spatial_ghost, both, p1, below, above],
        1,
        [one],
        2,
        56,
    )
    here, there, qs = lax.optimization_barrier((here, there, qs))
    qs = trade(qs)
    tables = gather_end(here, there)

    (chaos,) = call(
        functools.partial(table_body, n, slots),
        [shaped((modes, modes))],
        [where, chaos_targets, chaos_count, own] + tables,
        3,
    )
    slab = shaped((n, rows, width), F32)
    double = shaped((n, 2 * rows, width))
    w0, c1, ca0, *ws = call(
        functools.partial(stage_a, n),
        [slab, slab, slab] + sent(2),
        [where] + ps + [chaos, mean_inverse],
        1,
        [double, shaped((n, rows, width))],
    )
    ws = trade(ws)
    tile = shaped((devices, 128), F32)
    *vs, v1, held, sums = call(
        functools.partial(stage_b, n),
        sent(1) + [slab, slab, tile],
        [where] + qs + [chaos, mean_inverse, w0, c1, ca0],
        1,
        [double, double],
    )
    vs = trade(vs)
    *xs, dots = call(
        functools.partial(stage_c, n),
        sent(1) + [tile],
        [where, chaos, mean_inverse, w0, v1, held, sums],
        1,
        [shaped((n, rows, width))] * 2,
    )
    dots, xs, ws = lax.optimization_barrier((dots, xs, ws))
    xs = trade(xs)
    dots = lax.all_to_all(dots, ("space", "mode"), split_axis=0, concat_axis=0, tiled=True)
    (field,) = call(
        functools.partial(end_body, n, cells),
        [shaped((nodes, width), F32)],
        [where, guess, dots] + ws + vs + xs,
        1,
    )
    return field


def solution(mesh):
    placed = (
        P("space", "mode"),
        P("space", "mode"),
        P("space", None),
        P("space", None),
        P("space", None),
        P("mode", None, None),
        P(),
        P(),
        P(),
    )
    return jax.shard_map(
        shards, mesh=mesh, in_specs=placed, out_specs=P("space", "mode"), check_vma=False
    )
```

```python
import functools

import jax
import jax.numpy as jnp
from jax import lax
from jax.experimental import pallas as pl
from jax.experimental.pallas import tpu as pltpu
from jax.sharding import PartitionSpec as P


step_gain = 0.5
F32 = jnp.float32
BF16 = jnp.bfloat16
VMEM = pl.BlockSpec(memory_space=pltpu.VMEM)
SMEM = pl.BlockSpec(memory_space=pltpu.SMEM)


def call(body, outs, args, scalars=0, scratch=(), limit=16):
    return pl.pallas_call(
        body,
        out_shape=outs,
        in_specs=[SMEM] * scalars + [VMEM] * (len(args) - scalars),
        out_specs=[VMEM] * len(outs),
        scratch_shapes=[pltpu.VMEM(leaf.shape, leaf.dtype) for leaf in scratch],
        compiler_params=pltpu.CompilerParams(vmem_limit_bytes=limit << 20),
        cost_estimate=pl.CostEstimate(flops=1, bytes_accessed=1, transcendentals=0),
    )(*args)


def shaped(shape, dtype=BF16):
    return jax.ShapeDtypeStruct(shape, dtype)


def rows_of(owner, rows):
    return pl.ds(pl.multiple_of(owner * rows, rows), rows)


def mm(a, b):
    return jnp.dot(a, b, preferred_element_type=F32)


def mmt(a, b):
    return lax.dot_general(a, b, (((1,), (1,)), ((), ())), preferred_element_type=F32)


def flip_permute(x, axis, bit):
    return lax.ppermute(x, axis, [(i, i ^ bit) for i in range(lax.axis_size(axis))])


def trade(pieces):
    return [pieces[0]] + [flip_permute(p, "mode", k) for k, p in enumerate(pieces) if k > 0]


def swap(x):
    return lax.all_to_all(x, "mode", split_axis=0, concat_axis=0, tiled=True)


def halo(lower, upper):
    count = lax.axis_size("space")
    below = lax.ppermute(upper, "space", [(i, i + 1) for i in range(count - 1)])
    above = lax.ppermute(lower, "space", [(i + 1, i) for i in range(count - 1)])
    return below, above


def picked_rows(pick, x, lower, upper):
    ghost = lower.shape[0]
    rows = mm(pick[...], x).astype(BF16)
    lower[...] = rows[:ghost]
    upper[...] = rows[ghost:]


def start_body(u_ref, pick, whole, lower, upper):
    whole[...] = u_ref[...].astype(BF16)
    picked_rows(pick, whole[...], lower, upper)


def spatial_of(diag, ghostly, x, below, above):
    ghost = below.shape[0]
    y = mm(diag[...], x[...])
    y = y + mm(ghostly[:, :ghost], below[...])
    return y + mm(ghostly[:, ghost:], above[...])


def first_body(n, diag, ghostly, f_ref, x, below, above, pick, both, lower, upper, sent):
    nodes, width = x.shape
    rows = nodes // n
    s = spatial_of(diag, ghostly, x, below, above)
    p = f_ref[...] - s
    high = p.astype(BF16)
    low = (p - high.astype(F32)).astype(BF16)
    both[:, :width] = s.astype(BF16)
    both[:, width:] = high
    picked_rows(pick, both[...], lower, upper)
    for k in range(n):
        at = slice(k * rows, (k + 1) * rows)
        sent[k, 0] = x[at, :]
        sent[k, 1] = high[at]
        sent[k, 2] = low[at]
        sent[k, 3] = both[at, :width]


def second_body(diag, ghostly, x, below, above, pick, both, p1, lower, upper):
    both[...] = spatial_of(diag, ghostly, x, below, above).astype(BF16)
    p1[...] = both[:, both.shape[1] // 2 :]
    picked_rows(pick, p1[...], lower, upper)


def third_body(n, where, diag, ghostly, both, x, below, above, *outs):
    rows = x.shape[0] // n
    width = x.shape[1]
    whole = outs[-1]
    whole[...] = spatial_of(diag, ghostly, x, below, above).astype(BF16)
    for k in range(n):
        at = rows_of(where[0] ^ k, rows)
        outs[k][0] = both[at, :width]
        outs[k][1] = x[at, :]
        outs[k][2] = whole[at, :]


def table_body(n, slots, where, targets, counts, own, here, beside, there, across, out):
    entries, width = own.shape[:2]
    per = entries // slots
    quarter = entries // 4
    step = 256

    def clear(i, carry):
        out[rows_of(i, step), :] = jnp.zeros((step, out.shape[1]), out.dtype)
        return carry

    lax.fori_loop(0, out.shape[0] // step, clear, 0)

    def fill(owner, base, count, get):
        def place(i, carry):
            entry = base + i
            source = owner * per + entry // slots
            slot = entry % slots

            @pl.when(slot < counts[source])
            def _():
                out[rows_of(source, width), rows_of(targets[source, slot], width)] = get(i)

            return carry

        lax.fori_loop(0, count, place, 0, unroll=True)

    fill(where[0], 0, entries, lambda i: own[i])
    for at in range(n - 1):
        owner = lax.rem(where[0] + 1 + at, n)
        for which, ref in enumerate((here, beside, there, across)):
            fill(
                owner,
                (where[1] ^ which) * quarter,
                quarter,
                lambda i, ref=ref, at=at: ref[at, i],
            )


def by_table(n, me, get, table, emit):
    width = table.shape[0] // n
    for g in range(n):
        total = None
        for k in range(n):
            part = mm(get(k), table[rows_of(me ^ k, width), rows_of(me ^ g, width)])
            total = part if total is None else total + part
        emit(g, total)


def by_inverse(n, me, get, inverse, emit):
    width = inverse.shape[0] // n
    for g in range(n):
        total = None
        for k in range(n):
            part = mmt(get(k), inverse[rows_of(me ^ g, width), rows_of(me ^ k, width)])
            total = part if total is None else total + part
        emit(g, total)


def stage_a(n, where, ps, chaos, inverse, w0, c1, ca0, *refs):
    outs = refs[:n]
    pair, quick = refs[n:]
    me = where[0]
    rows = w0.shape[1]

    def residual(g, value):
        r = ps[me ^ g, 1].astype(F32) + ps[me ^ g, 2].astype(F32) - value[:rows]
        high = r.astype(BF16)
        pair[g, :rows] = high
        pair[g, rows:] = (r - high.astype(F32)).astype(BF16)
        c1[g] = value[rows:]

    by_table(n, me, lambda k: jnp.concatenate([ps[me ^ k, 0], ps[me ^ k, 3]], axis=0), chaos, residual)

    def updated(g, value):
        w = value[:rows] + value[rows:]
        w0[g] = w
        high = w.astype(BF16)
        quick[g] = high
        outs[g][0] = high
        outs[g][1] = (w - high.astype(F32)).astype(BF16)

    by_inverse(n, me, lambda k: pair[k], inverse, updated)

    def coupled(g, value):
        ca0[g] = value

    by_table(n, me, lambda k: quick[k], chaos, coupled)


def stage_b(n, where, *refs):
    qs = refs[:n]
    chaos, inverse, w0, c1, ca0 = refs[n : n + 5]
    outs = refs[n + 5 : 2 * n + 5]
    v1, held, sums_out, pair, more = refs[2 * n + 5 :]
    me = where[0]
    rows = w0.shape[1]
    for g in range(n):
        pair[g, :rows] = (qs[g][1].astype(F32) - c1[g]).astype(BF16)

    def residual(g, value):
        pair[g, rows:] = (qs[g][2].astype(F32) - value).astype(BF16)

    by_table(n, me, lambda k: qs[k][0], chaos, residual)

    def moved(g, value):
        more[g, :rows] = value[:rows].astype(BF16)
        held[g] = value[rows:]
        more[g, rows:] = (value[:rows] + ca0[g]).astype(BF16)

    by_inverse(n, me, lambda k: pair[k], inverse, moved)

    def coupled(g, value):
        pair[g, :rows] = more[g, rows:]
        pair[g, rows:] = (held[g] + value).astype(BF16)

    by_table(n, me, lambda k: more[k, :rows], chaos, coupled)
    sums = [0.0] * 3

    def first(g, value):
        v = value[:rows]
        v1[g] = v
        outs[g][0] = v.astype(BF16)
        held[g] = value[rows:]
        sums[0] += jnp.sum(w0[g] * w0[g])
        sums[1] += jnp.sum(w0[g] * v)
        sums[2] += jnp.sum(v * v)

    by_inverse(n, me, lambda k: pair[k], inverse, first)
    lanes_of(sums_out, sums, 0)


def lanes_of(out, sums, base):
    lane = lax.broadcasted_iota(jnp.int32, out.shape, 2)
    row = jnp.zeros(out.shape, F32)
    for at, value in enumerate(sums):
        row = jnp.where(lane == base + at, value, row)
    out[...] = row


def stage_c(n, where, chaos, inverse, w0, v1, held, sums_in, *refs):
    outs = refs[:n]
    dots, one, two = refs[n:]
    me = where[0]
    for g in range(n):
        one[g] = v1[g].astype(BF16)

    def last_in(g, value):
        two[g] = (held[g] + value).astype(BF16)

    by_table(n, me, lambda k: one[k], chaos, last_in)
    sums = [0.0] * 3

    def second(g, value):
        outs[g][0] = value.astype(BF16)
        sums[0] += jnp.sum(w0[g] * value)
        sums[1] += jnp.sum(v1[g] * value)
        sums[2] += jnp.sum(value * value)

    by_inverse(n, me, lambda k: two[k], inverse, second)
    lanes_of(dots, sums, 3)
    dots[...] = dots[...] + sums_in[...]


def end_body(n, cells, where, u_ref, dots, *refs):
    ws, vs, xs, out = refs[:n], refs[n : 2 * n], refs[2 * n : 3 * n], refs[3 * n]
    rows = u_ref.shape[0] // n
    means = jnp.sum(dots[...], axis=0)[:1] / cells
    lane = lax.broadcasted_iota(jnp.int32, means.shape, 1)
    g00, g01, g11, g02, g12, g22 = [
        jnp.sum(jnp.where(lane == at, means, 0.0), axis=1, keepdims=True) for at in range(6)
    ]

    def damping(mean):
        return step_gain / jnp.sqrt(jnp.maximum(mean, 0.0) + 1e-06)

    d0 = damping(g00)
    d1 = damping(g00 - 2.0 * d0 * g01 + d0 * d0 * g11)
    a, b = d0 + d1, d0 * d1
    d2 = damping(
        g00 + a * a * g11 + b * b * g22 - 2.0 * a * g01 + 2.0 * b * g02 - 2.0 * a * b * g12
    )
    x0 = d0 + d1 + d2
    x1 = -(d1 * d0 + d2 * a)
    x2 = d2 * b
    for k in range(n):
        at = rows_of(where[0] ^ k, rows)
        w = ws[k][0].astype(F32) + ws[k][1].astype(F32)
        moved = x0 * w + x1 * vs[k][0].astype(F32) + x2 * xs[k][0].astype(F32)
        out[at, :] = u_ref[at, :] + moved


def shards(
    guess,
    forcing,
    spatial_diag,
    spatial_ghost,
    ghost_rows,
    chaos_vals,
    chaos_targets,
    chaos_count,
    mean_inverse,
):
    n = lax.axis_size("mode")
    devices = n * lax.axis_size("space")
    nodes, width = guess.shape
    rows = nodes // n
    ghost = ghost_rows.shape[1]
    modes = mean_inverse.shape[0]
    slots = chaos_targets.shape[1]
    cells = float(nodes * width * devices)
    me = lax.axis_index("mode").astype(jnp.int32)
    quarter = (lax.axis_index("space") % 4).astype(jnp.int32)
    where = jnp.stack([me, quarter])
    pick = (ghost_rows.reshape(-1)[:, None] == jnp.arange(nodes, dtype=jnp.int32)[None, :]).astype(
        BF16
    )

    def sent(count):
        return [shaped((count, rows, width))] * n

    def edges(times):
        return [shaped((ghost, times * width))] * 2

    one, two = shaped((nodes, width)), shaped((nodes, 2 * width))
    square = shaped((modes, modes))
    own = jnp.swapaxes(chaos_vals, 1, 2)
    share = own.shape[0] // 4
    mine = lax.dynamic_slice_in_dim(own, quarter * share, share, 0)
    here = swap(jnp.broadcast_to(mine[None], (n,) + mine.shape))
    here = lax.dynamic_slice_in_dim(jnp.concatenate([here, here], axis=0), me + 1, n - 1, 0)
    whole, lower, upper = call(start_body, [one] + edges(1), [guess, pick])
    below, above = halo(lower, upper)
    own, below, above = lax.optimization_barrier((own, below, above))
    both, lower, upper, ps = call(
        functools.partial(first_body, n),
        [two] + edges(2) + [shaped((n, 4, rows, width))],
        [spatial_diag, spatial_ghost, forcing, whole, below, above, pick],
    )
    below, above = halo(lower, upper)
    ps = swap(ps)
    here, below, above = lax.optimization_barrier((here, below, above))
    there = flip_permute(here, "space", 2)
    both, p1, lower, upper = call(
        second_body,
        [two, one] + edges(1),
        [spatial_diag, spatial_ghost, both, below, above, pick],
    )
    below, above = halo(lower, upper)
    qs = call(
        functools.partial(third_body, n),
        sent(3),
        [where, spatial_diag, spatial_ghost, both, p1, below, above],
        1,
        [one],
    )
    there, qs = lax.optimization_barrier((there, qs))
    qs = trade(qs)
    beside, across = flip_permute(here, "space", 1), flip_permute(there, "space", 1)
    across, ps = lax.optimization_barrier((across, ps))
    (chaos,) = call(
        functools.partial(table_body, n, slots),
        [square],
        [where, chaos_targets, chaos_count, own, here, beside, there, across],
        3,
    )
    slab = shaped((n, rows, width), F32)
    double = shaped((n, 2 * rows, width))
    w0, c1, ca0, *ws = call(
        functools.partial(stage_a, n),
        [slab, slab, slab] + sent(2),
        [where, ps, chaos, mean_inverse],
        1,
        [double, shaped((n, rows, width))],
    )
    ws = trade(ws)
    tile = shaped((devices, 8, 128), F32)
    *vs, v1, held, sums = call(
        functools.partial(stage_b, n),
        sent(1) + [slab, slab, tile],
        [where] + qs + [chaos, mean_inverse, w0, c1, ca0],
        1,
        [double, double],
    )
    vs = trade(vs)
    *xs, dots = call(
        functools.partial(stage_c, n),
        sent(1) + [tile],
        [where, chaos, mean_inverse, w0, v1, held, sums],
        1,
        [shaped((n, rows, width))] * 2,
    )
    dots, xs, ws = lax.optimization_barrier((dots, xs, ws))
    xs = trade(xs)
    dots = lax.all_to_all(dots, ("space", "mode"), split_axis=0, concat_axis=0, tiled=True)
    (field,) = call(
        functools.partial(end_body, n, cells),
        [shaped((nodes, width), F32)],
        [where, guess, dots] + ws + vs + xs,
        1,
    )
    return field


def solution(mesh):
    placed = (
        P("space", "mode"),
        P("space", "mode"),
        P("space", None),
        P("space", None),
        P("space", None),
        P("mode", None, None),
        P(),
        P(),
        P(),
    )
    return jax.shard_map(
        shards, mesh=mesh, in_specs=placed, out_specs=P("space", "mode"), check_vma=False
    )
```

```python
import functools

import jax
import jax.numpy as jnp
from jax import lax
from jax.experimental import pallas as pl
from jax.experimental.pallas import tpu as pltpu
from jax.sharding import PartitionSpec as P


step_gain = 0.5
F32 = jnp.float32
BF16 = jnp.bfloat16
VMEM = pl.BlockSpec(memory_space=pltpu.VMEM)
SMEM = pl.BlockSpec(memory_space=pltpu.SMEM)


def call(body, outs, args, scalars=0, scratch=(), limit=16):
    return pl.pallas_call(
        body,
        out_shape=outs,
        in_specs=[SMEM] * scalars + [VMEM] * (len(args) - scalars),
        out_specs=[VMEM] * len(outs),
        scratch_shapes=[pltpu.VMEM(leaf.shape, leaf.dtype) for leaf in scratch],
        compiler_params=pltpu.CompilerParams(vmem_limit_bytes=limit << 20),
        cost_estimate=pl.CostEstimate(flops=1, bytes_accessed=1, transcendentals=0),
    )(*args)


def shaped(shape, dtype=BF16):
    return jax.ShapeDtypeStruct(shape, dtype)


def rows_of(owner, rows):
    return pl.ds(pl.multiple_of(owner * rows, rows), rows)


def mm(a, b):
    return jnp.dot(a, b, preferred_element_type=F32)


def mmt(a, b):
    return lax.dot_general(a, b, (((1,), (1,)), ((), ())), preferred_element_type=F32)


def flip_permute(x, axis, bit):
    return lax.ppermute(x, axis, [(i, i ^ bit) for i in range(lax.axis_size(axis))])


def trade(pieces):
    return [pieces[0]] + [flip_permute(p, "mode", k) for k, p in enumerate(pieces) if k > 0]


def swap(x):
    return lax.all_to_all(x, "mode", split_axis=0, concat_axis=0, tiled=True)


def halo(lower, upper):
    count = lax.axis_size("space")
    below = lax.ppermute(upper, "space", [(i, i + 1) for i in range(count - 1)])
    above = lax.ppermute(lower, "space", [(i + 1, i) for i in range(count - 1)])
    return below, above


def picked_rows(pick, x, lower, upper):
    ghost = lower.shape[0]
    rows = mm(pick[...], x).astype(BF16)
    lower[...] = rows[:ghost]
    upper[...] = rows[ghost:]


def start_body(u_ref, pick, whole, lower, upper):
    whole[...] = u_ref[...].astype(BF16)
    picked_rows(pick, whole[...], lower, upper)


def spatial_of(diag, ghostly, x, below, above):
    ghost = below.shape[0]
    y = mm(diag[...], x[...])
    y = y + mm(ghostly[:, :ghost], below[...])
    return y + mm(ghostly[:, ghost:], above[...])


def first_body(n, diag, ghostly, f_ref, x, below, above, pick, both, lower, upper, sent):
    nodes, width = x.shape
    rows = nodes // n
    s = spatial_of(diag, ghostly, x, below, above)
    p = f_ref[...] - s
    high = p.astype(BF16)
    low = (p - high.astype(F32)).astype(BF16)
    both[:, :width] = s.astype(BF16)
    both[:, width:] = high
    picked_rows(pick, both[...], lower, upper)
    for k in range(n):
        at = slice(k * rows, (k + 1) * rows)
        sent[k, 0] = x[at, :]
        sent[k, 1] = high[at]
        sent[k, 2] = low[at]
        sent[k, 3] = both[at, :width]


def second_body(diag, ghostly, x, below, above, pick, both, p1, lower, upper):
    both[...] = spatial_of(diag, ghostly, x, below, above).astype(BF16)
    p1[...] = both[:, both.shape[1] // 2 :]
    picked_rows(pick, p1[...], lower, upper)


def third_body(n, where, diag, ghostly, both, x, below, above, *outs):
    rows = x.shape[0] // n
    width = x.shape[1]
    whole = outs[-1]
    whole[...] = spatial_of(diag, ghostly, x, below, above).astype(BF16)
    for k in range(n):
        at = rows_of(where[0] ^ k, rows)
        outs[k][0] = both[at, :width]
        outs[k][1] = x[at, :]
        outs[k][2] = whole[at, :]


def table_body(n, slots, where, targets, counts, own, here, beside, there, across, out):
    entries, width = own.shape[:2]
    per = entries // slots
    quarter = entries // 4
    step = 256

    def clear(i, carry):
        out[rows_of(i, step), :] = jnp.zeros((step, out.shape[1]), out.dtype)
        return carry

    lax.fori_loop(0, out.shape[0] // step, clear, 0)

    def fill(owner, base, count, get):
        def place(i, carry):
            entry = base + i
            source = owner * per + entry // slots
            slot = entry % slots

            @pl.when(slot < counts[source])
            def _():
                out[rows_of(source, width), rows_of(targets[source, slot], width)] = get(i)

            return carry

        lax.fori_loop(0, count, place, 0, unroll=True)

    fill(where[0], 0, entries, lambda i: own[i])
    for at in range(n - 1):
        owner = lax.rem(where[0] + 1 + at, n)
        for which, ref in enumerate((here, beside, there, across)):
            fill(
                owner,
                (where[1] ^ which) * quarter,
                quarter,
                lambda i, ref=ref, at=at: ref[at, i],
            )


def by_table(n, me, get, table, emit):
    width = table.shape[0] // n
    for g in range(n):
        total = None
        for k in range(n):
            part = mm(get(k), table[rows_of(me ^ k, width), rows_of(me ^ g, width)])
            total = part if total is None else total + part
        emit(g, total)


def by_inverse(n, me, get, inverse, emit):
    width = inverse.shape[0] // n
    for g in range(n):
        total = None
        for k in range(n):
            part = mmt(get(k), inverse[rows_of(me ^ g, width), rows_of(me ^ k, width)])
            total = part if total is None else total + part
        emit(g, total)


def stage_a(n, where, ps, chaos, inverse, w0, c1, ca0, *refs):
    outs = refs[:n]
    pair, quick = refs[n:]
    me = where[0]
    rows = w0.shape[1]

    def residual(g, value):
        r = ps[me ^ g, 1].astype(F32) + ps[me ^ g, 2].astype(F32) - value[:rows]
        high = r.astype(BF16)
        pair[g, :rows] = high
        pair[g, rows:] = (r - high.astype(F32)).astype(BF16)
        c1[g] = value[rows:]

    by_table(n, me, lambda k: jnp.concatenate([ps[me ^ k, 0], ps[me ^ k, 3]], axis=0), chaos, residual)

    def updated(g, value):
        w = value[:rows] + value[rows:]
        w0[g] = w
        high = w.astype(BF16)
        quick[g] = high
        outs[g][0] = high
        outs[g][1] = (w - high.astype(F32)).astype(BF16)

    by_inverse(n, me, lambda k: pair[k], inverse, updated)

    def coupled(g, value):
        ca0[g] = value

    by_table(n, me, lambda k: quick[k], chaos, coupled)


def stage_b(n, where, *refs):
    qs = refs[:n]
    chaos, inverse, w0, c1, ca0 = refs[n : n + 5]
    outs = refs[n + 5 : 2 * n + 5]
    dots, v1, held, pair, more = refs[2 * n + 5 :]
    me = where[0]
    rows = w0.shape[1]
    for g in range(n):
        pair[g, :rows] = (qs[g][1].astype(F32) - c1[g]).astype(BF16)

    def residual(g, value):
        pair[g, rows:] = (qs[g][2].astype(F32) - value).astype(BF16)

    by_table(n, me, lambda k: qs[k][0], chaos, residual)

    def moved(g, value):
        more[g, :rows] = value[:rows].astype(BF16)
        held[g] = value[rows:]
        more[g, rows:] = (value[:rows] + ca0[g]).astype(BF16)

    by_inverse(n, me, lambda k: pair[k], inverse, moved)

    def coupled(g, value):
        pair[g, :rows] = more[g, rows:]
        pair[g, rows:] = (held[g] + value).astype(BF16)

    by_table(n, me, lambda k: more[k, :rows], chaos, coupled)
    sums = [0.0] * 6

    def first(g, value):
        v = value[:rows]
        v1[g] = v
        outs[g][0] = v.astype(BF16)
        held[g] = value[rows:]
        sums[0] += jnp.sum(w0[g] * w0[g])
        sums[1] += jnp.sum(w0[g] * v)
        sums[2] += jnp.sum(v * v)

    by_inverse(n, me, lambda k: pair[k], inverse, first)
    def last_in(g, value):
        more[g, :rows] = (held[g] + value).astype(BF16)

    by_table(n, me, lambda k: outs[k][0], chaos, last_in)

    def second(g, value):
        outs[g][1] = value.astype(BF16)
        sums[3] += jnp.sum(w0[g] * value)
        sums[4] += jnp.sum(v1[g] * value)
        sums[5] += jnp.sum(value * value)

    by_inverse(n, me, lambda k: more[k, :rows], inverse, second)
    lanes_of(dots, sums, 0)


def lanes_of(out, sums, base):
    lane = lax.broadcasted_iota(jnp.int32, out.shape, 2)
    row = jnp.zeros(out.shape, F32)
    for at, value in enumerate(sums):
        row = jnp.where(lane == base + at, value, row)
    out[...] = row


def end_body(n, cells, where, u_ref, dots, *refs):
    ws, vs, out = refs[:n], refs[n : 2 * n], refs[2 * n]
    rows = u_ref.shape[0] // n
    means = jnp.sum(dots[...], axis=0)[:1] / cells
    lane = lax.broadcasted_iota(jnp.int32, means.shape, 1)
    g00, g01, g11, g02, g12, g22 = [
        jnp.sum(jnp.where(lane == at, means, 0.0), axis=1, keepdims=True) for at in range(6)
    ]

    def damping(mean):
        return step_gain / jnp.sqrt(jnp.maximum(mean, 0.0) + 1e-06)

    d0 = damping(g00)
    d1 = damping(g00 - 2.0 * d0 * g01 + d0 * d0 * g11)
    a, b = d0 + d1, d0 * d1
    d2 = damping(
        g00 + a * a * g11 + b * b * g22 - 2.0 * a * g01 + 2.0 * b * g02 - 2.0 * a * b * g12
    )
    x0 = d0 + d1 + d2
    x1 = -(d1 * d0 + d2 * a)
    x2 = d2 * b
    for k in range(n):
        at = rows_of(where[0] ^ k, rows)
        w = ws[k][0].astype(F32) + ws[k][1].astype(F32)
        moved = x0 * w + x1 * vs[k][0].astype(F32) + x2 * vs[k][1].astype(F32)
        out[at, :] = u_ref[at, :] + moved


def shards(
    guess,
    forcing,
    spatial_diag,
    spatial_ghost,
    ghost_rows,
    chaos_vals,
    chaos_targets,
    chaos_count,
    mean_inverse,
):
    n = lax.axis_size("mode")
    devices = n * lax.axis_size("space")
    nodes, width = guess.shape
    rows = nodes // n
    ghost = ghost_rows.shape[1]
    modes = mean_inverse.shape[0]
    slots = chaos_targets.shape[1]
    cells = float(nodes * width * devices)
    me = lax.axis_index("mode").astype(jnp.int32)
    quarter = (lax.axis_index("space") % 4).astype(jnp.int32)
    where = jnp.stack([me, quarter])
    pick = (ghost_rows.reshape(-1)[:, None] == jnp.arange(nodes, dtype=jnp.int32)[None, :]).astype(
        BF16
    )

    def sent(count):
        return [shaped((count, rows, width))] * n

    def edges(times):
        return [shaped((ghost, times * width))] * 2

    one, two = shaped((nodes, width)), shaped((nodes, 2 * width))
    square = shaped((modes, modes))
    own = jnp.swapaxes(chaos_vals, 1, 2)
    share = own.shape[0] // 4
    mine = lax.dynamic_slice_in_dim(own, quarter * share, share, 0)
    here = swap(jnp.broadcast_to(mine[None], (n,) + mine.shape))
    here = lax.dynamic_slice_in_dim(jnp.concatenate([here, here], axis=0), me + 1, n - 1, 0)
    whole, lower, upper = call(start_body, [one] + edges(1), [guess, pick])
    below, above = halo(lower, upper)
    own, below, above = lax.optimization_barrier((own, below, above))
    both, lower, upper, ps = call(
        functools.partial(first_body, n),
        [two] + edges(2) + [shaped((n, 4, rows, width))],
        [spatial_diag, spatial_ghost, forcing, whole, below, above, pick],
    )
    below, above = halo(lower, upper)
    ps = swap(ps)
    here, below, above = lax.optimization_barrier((here, below, above))
    there = flip_permute(here, "space", 2)
    both, p1, lower, upper = call(
        second_body,
        [two, one] + edges(1),
        [spatial_diag, spatial_ghost, both, below, above, pick],
    )
    below, above = halo(lower, upper)
    qs = call(
        functools.partial(third_body, n),
        sent(3),
        [where, spatial_diag, spatial_ghost, both, p1, below, above],
        1,
        [one],
    )
    there, qs = lax.optimization_barrier((there, qs))
    qs = trade(qs)
    beside, across = flip_permute(here, "space", 1), flip_permute(there, "space", 1)
    across, ps = lax.optimization_barrier((across, ps))
    (chaos,) = call(
        functools.partial(table_body, n, slots),
        [square],
        [where, chaos_targets, chaos_count, own, here, beside, there, across],
        3,
    )
    slab = shaped((n, rows, width), F32)
    double = shaped((n, 2 * rows, width))
    w0, c1, ca0, *ws = call(
        functools.partial(stage_a, n),
        [slab, slab, slab] + sent(2),
        [where, ps, chaos, mean_inverse],
        1,
        [double, shaped((n, rows, width))],
    )
    ws = trade(ws)
    tile = shaped((devices, 8, 128), F32)
    *vs, dots = call(
        functools.partial(stage_b, n),
        sent(2) + [tile],
        [where] + qs + [chaos, mean_inverse, w0, c1, ca0],
        1,
        [slab, slab, double, double],
    )
    dots, vs, ws = lax.optimization_barrier((dots, vs, ws))
    vs = trade(vs)
    dots = lax.all_to_all(dots, ("space", "mode"), split_axis=0, concat_axis=0, tiled=True)
    (field,) = call(
        functools.partial(end_body, n, cells),
        [shaped((nodes, width), F32)],
        [where, guess, dots] + ws + vs,
        1,
    )
    return field


def solution(mesh):
    placed = (
        P("space", "mode"),
        P("space", "mode"),
        P("space", None),
        P("space", None),
        P("space", None),
        P("mode", None, None),
        P(),
        P(),
        P(),
    )
    return jax.shard_map(
        shards, mesh=mesh, in_specs=placed, out_specs=P("space", "mode"), check_vma=False
    )
```

```python
import functools

import jax
import jax.numpy as jnp
from jax import lax
from jax.experimental import pallas as pl
from jax.experimental.pallas import tpu as pltpu
from jax.sharding import PartitionSpec as P


step_gain = 0.5
F32 = jnp.float32
BF16 = jnp.bfloat16
VMEM = pl.BlockSpec(memory_space=pltpu.VMEM)
SMEM = pl.BlockSpec(memory_space=pltpu.SMEM)


def call(body, outs, args, scalars=0, scratch=(), limit=16):
    return pl.pallas_call(
        body,
        out_shape=outs,
        in_specs=[SMEM] * scalars + [VMEM] * (len(args) - scalars),
        out_specs=[VMEM] * len(outs),
        scratch_shapes=[pltpu.VMEM(leaf.shape, leaf.dtype) for leaf in scratch],
        compiler_params=pltpu.CompilerParams(vmem_limit_bytes=limit << 20),
        cost_estimate=pl.CostEstimate(flops=1, bytes_accessed=1, transcendentals=0),
    )(*args)


def shaped(shape, dtype=BF16):
    return jax.ShapeDtypeStruct(shape, dtype)


def rows_of(owner, rows):
    return pl.ds(pl.multiple_of(owner * rows, rows), rows)


def mm(a, b):
    return jnp.dot(a, b, preferred_element_type=F32)


def mmt(a, b):
    return lax.dot_general(a, b, (((1,), (1,)), ((), ())), preferred_element_type=F32)


def flip_permute(x, axis, bit):
    return lax.ppermute(x, axis, [(i, i ^ bit) for i in range(lax.axis_size(axis))])


def trade(pieces):
    return [pieces[0]] + [flip_permute(p, "mode", k) for k, p in enumerate(pieces) if k > 0]


def swap(x):
    return lax.all_to_all(x, "mode", split_axis=0, concat_axis=0, tiled=True)


def halo(lower, upper):
    count = lax.axis_size("space")
    below = lax.ppermute(upper, "space", [(i, i + 1) for i in range(count - 1)])
    above = lax.ppermute(lower, "space", [(i + 1, i) for i in range(count - 1)])
    return below, above


def picked_rows(pick, x, lower, upper):
    ghost = lower.shape[0]
    rows = mm(pick[...], x).astype(BF16)
    lower[...] = rows[:ghost]
    upper[...] = rows[ghost:]


def start_body(u_ref, pick, whole, lower, upper):
    whole[...] = u_ref[...].astype(BF16)
    picked_rows(pick, whole[...], lower, upper)


def spatial_of(diag, ghostly, x, below, above):
    ghost = below.shape[0]
    y = mm(diag[...], x[...])
    y = y + mm(ghostly[:, :ghost], below[...])
    return y + mm(ghostly[:, ghost:], above[...])


def first_body(n, diag, ghostly, f_ref, x, below, above, pick, both, lower, upper, sent):
    nodes, width = x.shape
    rows = nodes // n
    s = spatial_of(diag, ghostly, x, below, above)
    p = f_ref[...] - s
    high = p.astype(BF16)
    low = (p - high.astype(F32)).astype(BF16)
    both[:, :width] = s.astype(BF16)
    both[:, width:] = high
    picked_rows(pick, both[...], lower, upper)
    for k in range(n):
        at = slice(k * rows, (k + 1) * rows)
        sent[k, 0] = x[at, :]
        sent[k, 1] = high[at]
        sent[k, 2] = low[at]
        sent[k, 3] = both[at, :width]


def second_body(diag, ghostly, x, below, above, pick, both, p1, lower, upper):
    both[...] = spatial_of(diag, ghostly, x, below, above).astype(BF16)
    p1[...] = both[:, both.shape[1] // 2 :]
    picked_rows(pick, p1[...], lower, upper)


def third_body(n, where, diag, ghostly, both, x, below, above, *outs):
    rows = x.shape[0] // n
    width = x.shape[1]
    whole = outs[-1]
    whole[...] = spatial_of(diag, ghostly, x, below, above).astype(BF16)
    for k in range(n):
        at = rows_of(where[0] ^ k, rows)
        outs[k][0] = both[at, :width]
        outs[k][1] = x[at, :]
        outs[k][2] = whole[at, :]


def table_body(n, slots, where, targets, counts, own, here, beside, there, across, out):
    entries, width = own.shape[:2]
    per = entries // slots
    quarter = entries // 4
    step = 256

    def clear(i, carry):
        out[rows_of(i, step), :] = jnp.zeros((step, out.shape[1]), out.dtype)
        return carry

    lax.fori_loop(0, out.shape[0] // step, clear, 0)

    def fill(owner, base, count, get):
        def place(i, carry):
            entry = base + i
            source = owner * per + entry // slots
            slot = entry % slots

            @pl.when(slot < counts[source])
            def _():
                out[rows_of(source, width), rows_of(targets[source, slot], width)] = get(i)

            return carry

        lax.fori_loop(0, count, place, 0, unroll=True)

    fill(where[0], 0, entries, lambda i: own[i])
    for at in range(n - 1):
        owner = lax.rem(where[0] + 1 + at, n)
        for which, ref in enumerate((here, beside, there, across)):
            fill(
                owner,
                (where[1] ^ which) * quarter,
                quarter,
                lambda i, ref=ref, at=at: ref[at, i],
            )


def by_table(n, me, get, table, emit):
    width = table.shape[0] // n
    for g in range(n):
        total = None
        for k in range(n):
            part = mm(get(k), table[rows_of(me ^ k, width), rows_of(me ^ g, width)])
            total = part if total is None else total + part
        emit(g, total)


def by_inverse(n, me, get, inverse, emit):
    width = inverse.shape[0] // n
    for g in range(n):
        total = None
        for k in range(n):
            part = mmt(get(k), inverse[rows_of(me ^ g, width), rows_of(me ^ k, width)])
            total = part if total is None else total + part
        emit(g, total)


def stage_a(n, where, ps, chaos, inverse, w0, c1, ca0, *refs):
    outs = refs[:n]
    pair, quick = refs[n:]
    me = where[0]
    rows = w0.shape[1]

    def residual(g, value):
        r = ps[me ^ g, 1].astype(F32) + ps[me ^ g, 2].astype(F32) - value[:rows]
        high = r.astype(BF16)
        pair[g, :rows] = high
        pair[g, rows:] = (r - high.astype(F32)).astype(BF16)
        c1[g] = value[rows:]

    by_table(n, me, lambda k: jnp.concatenate([ps[me ^ k, 0], ps[me ^ k, 3]], axis=0), chaos, residual)

    def updated(g, value):
        w = value[:rows] + value[rows:]
        w0[g] = w
        high = w.astype(BF16)
        quick[g] = high
        outs[g][0] = high
        outs[g][1] = (w - high.astype(F32)).astype(BF16)

    by_inverse(n, me, lambda k: pair[k], inverse, updated)

    def coupled(g, value):
        ca0[g] = value

    by_table(n, me, lambda k: quick[k], chaos, coupled)


def table_and_a(
    n, slots, where, targets, counts, own, here, beside, there, across, ps, inverse, chaos, *refs
):
    table_body(n, slots, where, targets, counts, own, here, beside, there, across, chaos)
    stage_a(n, where, ps, chaos, inverse, *refs)


def stage_b(n, where, *refs):
    qs = refs[:n]
    chaos, inverse, w0, c1, ca0 = refs[n : n + 5]
    outs = refs[n + 5 : 2 * n + 5]
    dots, v1, held, pair, more = refs[2 * n + 5 :]
    me = where[0]
    rows = w0.shape[1]
    for g in range(n):
        pair[g, :rows] = (qs[g][1].astype(F32) - c1[g]).astype(BF16)

    def residual(g, value):
        pair[g, rows:] = (qs[g][2].astype(F32) - value).astype(BF16)

    by_table(n, me, lambda k: qs[k][0], chaos, residual)

    def moved(g, value):
        more[g, :rows] = value[:rows].astype(BF16)
        held[g] = value[rows:]
        more[g, rows:] = (value[:rows] + ca0[g]).astype(BF16)

    by_inverse(n, me, lambda k: pair[k], inverse, moved)

    def coupled(g, value):
        pair[g, :rows] = more[g, rows:]
        pair[g, rows:] = (held[g] + value).astype(BF16)

    by_table(n, me, lambda k: more[k, :rows], chaos, coupled)
    sums = [0.0] * 6

    def first(g, value):
        v = value[:rows]
        v1[g] = v
        outs[g][0] = v.astype(BF16)
        held[g] = value[rows:]
        sums[0] += jnp.sum(w0[g] * w0[g])
        sums[1] += jnp.sum(w0[g] * v)
        sums[2] += jnp.sum(v * v)

    by_inverse(n, me, lambda k: pair[k], inverse, first)
    def last_in(g, value):
        more[g, :rows] = (held[g] + value).astype(BF16)

    by_table(n, me, lambda k: outs[k][0], chaos, last_in)

    def second(g, value):
        value = value[:rows]
        outs[g][1] = value.astype(BF16)
        sums[3] += jnp.sum(w0[g] * value)
        sums[4] += jnp.sum(v1[g] * value)
        sums[5] += jnp.sum(value * value)

    by_inverse(n, me, lambda k: more[k], inverse, second)
    lanes_of(dots, sums, 0)


def lanes_of(out, sums, base):
    lane = lax.broadcasted_iota(jnp.int32, out.shape, 2)
    row = jnp.zeros(out.shape, F32)
    for at, value in enumerate(sums):
        row = jnp.where(lane == base + at, value, row)
    out[...] = row


def end_body(n, cells, where, u_ref, dots, *refs):
    ws, vs, out = refs[:n], refs[n : 2 * n], refs[2 * n]
    rows = u_ref.shape[0] // n
    means = jnp.sum(dots[...], axis=0)[:1] / cells
    lane = lax.broadcasted_iota(jnp.int32, means.shape, 1)
    g00, g01, g11, g02, g12, g22 = [
        jnp.sum(jnp.where(lane == at, means, 0.0), axis=1, keepdims=True) for at in range(6)
    ]

    def damping(mean):
        return step_gain / jnp.sqrt(jnp.maximum(mean, 0.0) + 1e-06)

    d0 = damping(g00)
    d1 = damping(g00 - 2.0 * d0 * g01 + d0 * d0 * g11)
    a, b = d0 + d1, d0 * d1
    d2 = damping(
        g00 + a * a * g11 + b * b * g22 - 2.0 * a * g01 + 2.0 * b * g02 - 2.0 * a * b * g12
    )
    x0 = d0 + d1 + d2
    x1 = -(d1 * d0 + d2 * a)
    x2 = d2 * b
    for k in range(n):
        at = rows_of(where[0] ^ k, rows)
        w = ws[k][0].astype(F32) + ws[k][1].astype(F32)
        moved = x0 * w + x1 * vs[k][0].astype(F32) + x2 * vs[k][1].astype(F32)
        out[at, :] = u_ref[at, :] + moved


def shards(
    guess,
    forcing,
    spatial_diag,
    spatial_ghost,
    ghost_rows,
    chaos_vals,
    chaos_targets,
    chaos_count,
    mean_inverse,
):
    n = lax.axis_size("mode")
    devices = n * lax.axis_size("space")
    nodes, width = guess.shape
    rows = nodes // n
    ghost = ghost_rows.shape[1]
    modes = mean_inverse.shape[0]
    slots = chaos_targets.shape[1]
    cells = float(nodes * width * devices)
    me = lax.axis_index("mode").astype(jnp.int32)
    quarter = (lax.axis_index("space") % 4).astype(jnp.int32)
    where = jnp.stack([me, quarter])
    pick = (ghost_rows.reshape(-1)[:, None] == jnp.arange(nodes, dtype=jnp.int32)[None, :]).astype(
        BF16
    )

    def sent(count):
        return [shaped((count, rows, width))] * n

    def edges(times):
        return [shaped((ghost, times * width))] * 2

    one, two = shaped((nodes, width)), shaped((nodes, 2 * width))
    square = shaped((modes, modes))
    own = jnp.swapaxes(chaos_vals, 1, 2)
    share = own.shape[0] // 4
    mine = lax.dynamic_slice_in_dim(own, quarter * share, share, 0)
    here = swap(jnp.broadcast_to(mine[None], (n,) + mine.shape))
    here = lax.dynamic_slice_in_dim(jnp.concatenate([here, here], axis=0), me + 1, n - 1, 0)
    whole, lower, upper = call(start_body, [one] + edges(1), [guess, pick])
    below, above = halo(lower, upper)
    own, below, above = lax.optimization_barrier((own, below, above))
    both, lower, upper, ps = call(
        functools.partial(first_body, n),
        [two] + edges(2) + [shaped((n, 4, rows, width))],
        [spatial_diag, spatial_ghost, forcing, whole, below, above, pick],
    )
    below, above = halo(lower, upper)
    ps = swap(ps)
    here, below, above = lax.optimization_barrier((here, below, above))
    there = flip_permute(here, "space", 2)
    both, p1, lower, upper = call(
        second_body,
        [two, one] + edges(1),
        [spatial_diag, spatial_ghost, both, below, above, pick],
    )
    below, above = halo(lower, upper)
    qs = call(
        functools.partial(third_body, n),
        sent(3),
        [where, spatial_diag, spatial_ghost, both, p1, below, above],
        1,
        [one],
    )
    there, qs = lax.optimization_barrier((there, qs))
    qs = trade(qs)
    beside, across = flip_permute(here, "space", 1), flip_permute(there, "space", 1)
    across, ps = lax.optimization_barrier((across, ps))
    slab = shaped((n, rows, width), F32)
    double = shaped((n, 2 * rows, width))
    chaos, w0, c1, ca0, *ws = call(
        functools.partial(table_and_a, n, slots),
        [square, slab, slab, slab] + sent(2),
        [where, chaos_targets, chaos_count, own, here, beside, there, across, ps, mean_inverse],
        3,
        [double, shaped((n, rows, width))],
    )
    ws = trade(ws)
    tile = shaped((devices, 8, 128), F32)
    *vs, dots = call(
        functools.partial(stage_b, n),
        sent(2) + [tile],
        [where] + qs + [chaos, mean_inverse, w0, c1, ca0],
        1,
        [slab, slab, double, double],
    )
    dots, vs, ws = lax.optimization_barrier((dots, vs, ws))
    vs = trade(vs)
    dots = lax.all_to_all(dots, ("space", "mode"), split_axis=0, concat_axis=0, tiled=True)
    (field,) = call(
        functools.partial(end_body, n, cells),
        [shaped((nodes, width), F32)],
        [where, guess, dots] + ws + vs,
        1,
    )
    return field


def solution(mesh):
    placed = (
        P("space", "mode"),
        P("space", "mode"),
        P("space", None),
        P("space", None),
        P("space", None),
        P("mode", None, None),
        P(),
        P(),
        P(),
    )
    return jax.shard_map(
        shards, mesh=mesh, in_specs=placed, out_specs=P("space", "mode"), check_vma=False
    )
```
